32 devices in a mesh: head: 4 (over y, core), req: 8 (over z, x).
Axes of the slice: x: 2, y: 2, z: 4, core: 2. Of those that a mesh axis runs over, the one named last changes fastest.
Arguments:
- learner_acceptance_matrix: float32 [2048, 2048], P(('head', 'req')), may hold values from -0.125 to 0.125
- learner_address_matrix: float32 [2048, 2048], P(('head', 'req')), may hold values from -0.125 to 0.125
- learner_content_matrix: float32 [2048, 2048], P(('head', 'req')), may hold values from -0.125 to 0.125
- learner_gating_matrix: float32 [2048, 2048], P(('head', 'req')), may hold values from -0.125 to 0.125
- learner_result_matrix: float32 [2048, 2048], P(('head', 'req')), may hold values from -0.125 to 0.125
- fading_narrowing_matrix: bfloat16 [2048, 64], replicated, may hold values from -0.125 to 0.125
- fading_widening_matrix: bfloat16 [64, 2048], P(None, 'head'), may hold values from -0.75 to 0.75
- feature_fading_speed: float32 [2048], P('head'), may hold values from 0.001 to 0.5
- current_reward: float32 [2048], P('head'), may hold values from -1 to 1
- symbol_blending_factors: float32 [5, 2048], replicated, may hold values from 0 to 1
- group_scaling_factor: float32 [2048], P('head'), may hold values from 0.5 to 1.5
- group_scaling_offset: float32 [2048], P('head'), may hold values from -1.75 to 1.75
- request_hidden_entries: bfloat16 [16, 512, 2048], P('req', None, 'head'), may hold values from -6 to 6
- request_valid_count: int32 [16], P('req'), may hold values from 1 to 512, 6144 in all
- request_destination_place: int32 [16], P('req'), may hold values from 0 to 511, as said below
- newest_symbol_hidden: bfloat16 [512, 2048], P('req', 'head'), may hold values from -6 to 6
- preceding_hidden_entry: bfloat16 [512, 2048], P('req', 'head'), may hold values from -6 to 6
- place_memory_matrix: float32 [512, 32, 64, 64], P('req', 'head'), may hold values from -6 to 6
- place_newness_marks: int32 [512], P('req'), may hold values 0 or 1
Outputs:
- prompt_hidden: bfloat16 [16, 512, 2048], P('req', None, 'head')
- decode_hidden: bfloat16 [512, 2048], P('req', 'head')
- new_state: float32 [512, 32, 64, 64], P('req', 'head')
- new_shift: bfloat16 [512, 2048], P('req', 'head')
The draws below stay inside these ranges and needn't reach their ends.
Inputs may be any that keep to these rules, and one draw needn't show every extreme that they name: Prompt p's slot is one of the 64 slots of the same index of req as prompt p, that is p // 2 == request_destination_place[p] // 64; the slots are distinct. `request_valid_count`: the longest prompt has exactly 512 live tokens.
All inputs are finite; a program needn't handle non-finite values. No bound on the sum of `request_valid_count` or of `place_newness_marks` on one device may be relied on, other than what follows from the above.
Results may differ from the reference program's by a relative error of at most 0.033.
Values may be sent and summed in bfloat16 or wider, within the bound.
A program may use at most 256 MiB of HBM per device.

```python
import math
import jax
import jax.numpy as jnp
import numpy as np
from jax import lax

EMBEDDING_SIZE = 2048
H = 32
HS = 64
DECAY_RANK = 64
L = 512
PROMPT_DEV = 2
REQ_DEV = 64
PROMPTS = 16
SLOTS = 512
N_HEAD = 4
N_REQ = 8


def draw_request_destination_place(key, part):
    devices = PROMPTS // PROMPT_DEV
    key_list = jax.random.split(jax.random.fold_in(key, 7), devices)
    orders = jax.vmap(lambda single_key: jax.random.permutation(single_key, REQ_DEV))(key_list)
    targets = jax.random.randint(jax.random.fold_in(key, 11), (devices,), 0, REQ_DEV)
    targets = targets.at[0].set(0).at[devices - 1].set(REQ_DEV - 1)
    chosen = orders[:, :PROMPT_DEV]
    offsets = (chosen - chosen[:, :1] + targets[:, None]) % REQ_DEV
    base_rows = jnp.arange(devices, dtype=jnp.int32)[:, None] * REQ_DEV
    return (base_rows + offsets).reshape(PROMPTS).astype(jnp.int32)


def set_ends(result, stream_key, least, high):
    place = [jax.random.randint(jax.random.fold_in(stream_key, axis), (), 0, length) for axis, length in enumerate(result.shape)]
    main_axis = result.shape.index(max(result.shape))
    neighbour = place[:main_axis] + [(place[main_axis] + 1) % result.shape[main_axis]] + place[main_axis + 1:]
    return result.at[tuple(place)].set(least).at[tuple(neighbour)].set(high)


def block_scale(key, extent, cuts, low, top_value):
    def one(dim, shards_of):
        steps = jax.random.uniform(jax.random.fold_in(jax.random.fold_in(key, 6), dim), (shards_of,), jnp.float32, low / len(cuts), top_value / len(cuts))
        return jnp.repeat(jnp.exp(steps), extent[dim] // shards_of).reshape((-1,) + (1,) * (len(extent) - dim - 1))

    level = one(*cuts[0])
    for cut in cuts[1:]:
        level = level * one(*cut)
    return level


def split_up(number_of, total, bound, slope):
    weights = [(1 << 20) // math.isqrt(rank ** slope) + 1 for rank in range(2, number_of + 1)]
    rest, counts = total - bound - (number_of - 1), [1] * (number_of - 1)
    while rest > 0:
        candidates = [i for i in range(number_of - 1) if counts[i] < bound]
        whole, budget = sum([weights[i] for i in candidates]), rest
        for i in candidates:
            more = min(bound - counts[i], max(1, budget * weights[i] // whole), rest)
            counts[i] = counts[i] + more
            rest = rest - more
    return np.array([bound] + counts)


def ragged_sizes(stream_key, count, total, most, lean):
    if count == 2:
        one = jax.random.randint(stream_key, (), max(1, total - most), min(most, total - 1) + 1)
        return jnp.stack([one, total - one])
    sizes = jnp.asarray(split_up(count, total, most, lean), jnp.int32)
    pairs = (count - 1) // 2
    donor, taker = sizes[1:1 + 2 * pairs:2], sizes[2:2 + 2 * pairs:2]
    room = jnp.minimum(donor - 1, most - taker)
    shifted = jax.random.randint(jax.random.fold_in(stream_key, 1), (pairs,), 0, 1 << 20) % (room + 1)
    sizes = sizes.at[1:1 + 2 * pairs:2].set(donor - shifted).at[2:2 + 2 * pairs:2].set(taker + shifted)
    return sizes[jax.random.permutation(jax.random.fold_in(stream_key, 2), count)]


def gaussian(stream_key, dims, deviation, limit, cuts=(), kind=jnp.bfloat16):
    drawn = deviation * jax.random.normal(stream_key, dims, jnp.float32)
    if cuts:
        drawn = drawn * block_scale(stream_key, dims, cuts, -0.22, 0.18)
    return jnp.clip(drawn, -limit, limit).astype(kind)


def setup_inputs(seed: int = 0) -> dict:
    keys = jax.random.split(jax.random.key(seed), 20)
    return {
        "learner_acceptance_matrix": gaussian(keys[0], (EMBEDDING_SIZE, EMBEDDING_SIZE), EMBEDDING_SIZE ** -0.5, 0.125, ((0, 32),), jnp.float32),
        "learner_address_matrix": gaussian(keys[1], (EMBEDDING_SIZE, EMBEDDING_SIZE), EMBEDDING_SIZE ** -0.5, 0.125, ((0, 32),), jnp.float32),
        "learner_content_matrix": gaussian(keys[2], (EMBEDDING_SIZE, EMBEDDING_SIZE), EMBEDDING_SIZE ** -0.5, 0.125, ((0, 32),), jnp.float32),
        "learner_gating_matrix": gaussian(keys[3], (EMBEDDING_SIZE, EMBEDDING_SIZE), EMBEDDING_SIZE ** -0.5, 0.125, ((0, 32),), jnp.float32),
        "learner_result_matrix": gaussian(keys[4], (EMBEDDING_SIZE, EMBEDDING_SIZE), EMBEDDING_SIZE ** -0.5, 0.125, ((0, 32),), jnp.float32),
        "fading_narrowing_matrix": gaussian(keys[5], (EMBEDDING_SIZE, DECAY_RANK), EMBEDDING_SIZE ** -0.5, 0.125),
        "fading_widening_matrix": gaussian(keys[6], (DECAY_RANK, EMBEDDING_SIZE), DECAY_RANK ** -0.5, 0.75, ((1, 4),)),
        "feature_fading_speed": jnp.clip(jnp.exp(math.log(0.5) - 6.214608 * jax.random.uniform(keys[7], (EMBEDDING_SIZE,), jnp.float32) ** block_scale(keys[7], (EMBEDDING_SIZE,), ((0, 4),), -0.2, 0.2)), 0.001, 0.5),
        "current_reward": jnp.clip(jax.random.uniform(keys[8], (EMBEDDING_SIZE,), jnp.float32, -1.0, 1.0) * block_scale(keys[8], (EMBEDDING_SIZE,), ((0, 4),), -0.4, 0.0), -1.0, 1.0),
        "symbol_blending_factors": jnp.clip(jax.random.uniform(keys[9], (5, EMBEDDING_SIZE), jnp.float32, 0.0, 1.0), 0.0, 1.0),
        "group_scaling_factor": jnp.clip(1.0 + 0.1 * jax.random.normal(keys[10], (EMBEDDING_SIZE,), jnp.float32), 0.5, 1.5),
        "group_scaling_offset": gaussian(keys[11], (EMBEDDING_SIZE,), 0.3, 1.75, ((0, 4),), jnp.float32),
        "request_hidden_entries": gaussian(keys[12], (PROMPTS, L, EMBEDDING_SIZE), 1.0, 6.0, ((0, 8), (2, 4))),
        "request_valid_count": ragged_sizes(keys[13], PROMPTS, PROMPTS * L * 3 // 4, L, 1).astype(jnp.int32),
        "request_destination_place": draw_request_destination_place(jax.random.fold_in(keys[19], 71), 0),
        "newest_symbol_hidden": gaussian(keys[15], (SLOTS, EMBEDDING_SIZE), 1.0, 6.0, ((0, 8), (1, 4))),
        "preceding_hidden_entry": gaussian(keys[16], (SLOTS, EMBEDDING_SIZE), 1.0, 6.0, ((0, 8), (1, 4))),
        "place_memory_matrix": gaussian(keys[17], (SLOTS, H, HS, HS), 1.0, 6.0, ((0, 8), (1, 4)), jnp.float32),
        "place_newness_marks": set_ends((jax.random.randint(keys[18], (SLOTS,), 0, 4) < 1).astype(jnp.int32), jax.random.fold_in(keys[18], 1), 0, 1),
    }


NORM_EPS = 0.00064

def project(left, right):
    return jnp.dot(left, right, preferred_element_type=jnp.float32)

def make_inputs(present, earlier, symbol_blending_factors, w_recept, w_key, w_value, w_gate, fading_narrowing_matrix, fading_widening_matrix, feature_fading_speed):
    current = present.astype(jnp.float32)
    previous = earlier.astype(jnp.float32)
    mixed_rows = [(current + (previous - current) * symbol_blending_factors[number]).astype(jnp.bfloat16) for number in range(5)]
    acceptance_entries = project(mixed_rows[0], w_recept).astype(jnp.bfloat16)
    address_entry_tile = project(mixed_rows[1], w_key).astype(jnp.bfloat16)
    content_entries = project(mixed_rows[2], w_value).astype(jnp.bfloat16)
    lowrank = jnp.tanh(project(mixed_rows[3], fading_narrowing_matrix)).astype(jnp.bfloat16)
    fading_exponent_log = -feature_fading_speed * jnp.exp(project(lowrank, fading_widening_matrix))
    gate_rows = jax.nn.silu(project(mixed_rows[4], w_gate))
    return (acceptance_entries.astype(jnp.float32), address_entry_tile.astype(jnp.float32), content_entries.astype(jnp.float32), fading_exponent_log, gate_rows)

def group_norm(outputs, group_scaling_factor, group_scaling_offset, gate_rows):
    center = outputs - lax.optimization_barrier(jnp.mean(outputs, axis=-1, keepdims=True))
    spread = lax.optimization_barrier(jnp.mean(center * center, axis=-1, keepdims=True))
    normed = (center / jnp.sqrt(spread + NORM_EPS)).reshape(outputs.shape[0], -1)
    return ((normed * group_scaling_factor + group_scaling_offset) * gate_rows).astype(jnp.bfloat16)

def head_sum(normed, w_output):
    block_width = normed.shape[1] // N_HEAD
    running = jnp.zeros((normed.shape[0], w_output.shape[1]), jnp.float32)
    for group_index in range(N_HEAD):
        lower_col = group_index * block_width
        partial_sum = project(normed[:, lower_col:lower_col + block_width], w_output[lower_col:lower_col + block_width])
        rounded = lax.optimization_barrier(partial_sum.astype(jnp.bfloat16))
        running = running + rounded.astype(jnp.float32)
    return running

def reference(learner_acceptance_matrix, learner_address_matrix, learner_content_matrix, learner_gating_matrix, learner_result_matrix, fading_narrowing_matrix, fading_widening_matrix, feature_fading_speed, current_reward, symbol_blending_factors, group_scaling_factor, group_scaling_offset, request_hidden_entries, request_valid_count, request_destination_place, newest_symbol_hidden, preceding_hidden_entry, place_memory_matrix, place_newness_marks):
    w_recept = learner_acceptance_matrix.astype(jnp.bfloat16)
    w_key = learner_address_matrix.astype(jnp.bfloat16)
    w_value = learner_content_matrix.astype(jnp.bfloat16)
    w_gate = learner_gating_matrix.astype(jnp.bfloat16)
    w_output = learner_result_matrix.astype(jnp.bfloat16)
    prompt_count, length, model_width = request_hidden_entries.shape
    group_count_all, group_breadth = (place_memory_matrix.shape[1], place_memory_matrix.shape[2])
    group_reward = current_reward.reshape(group_count_all, group_breadth)
    earlier = jnp.concatenate([jnp.zeros_like(request_hidden_entries[:, :1]), request_hidden_entries[:, :-1]], axis=1)
    acceptance_entries, address_entry_tile, content_entries, fading_exponent_log, gate_rows = make_inputs(request_hidden_entries.reshape(-1, model_width), earlier.reshape(-1, model_width), symbol_blending_factors, w_recept, w_key, w_value, w_gate, fading_narrowing_matrix, fading_widening_matrix, feature_fading_speed)
    positions = lax.broadcasted_iota(jnp.int32, (prompt_count, length), 1)
    live_mask = (positions < request_valid_count[:, None]).astype(jnp.float32).reshape(-1, 1)
    address_entry_tile = address_entry_tile * live_mask
    fading_exponent_log = fading_exponent_log * live_mask

    def shaped(array):
        return array.reshape(prompt_count, length, group_count_all, group_breadth).transpose(1, 0, 2, 3)

    def advance(running_memory, inputs):
        acceptance_array, address_array, content_array, w = inputs
        dyadic_matrix = address_array[..., :, None] * content_array[..., None, :]
        result_entry_amount = jnp.einsum('rnu,rnux->rnx', acceptance_array, running_memory + group_reward[..., :, None] * dyadic_matrix, precision=lax.Precision.HIGHEST)
        next_state = jnp.exp(w)[..., None] * running_memory + dyadic_matrix
        return (next_state, result_entry_amount)
    start_state = jnp.zeros((prompt_count, group_count_all, group_breadth, group_breadth), jnp.float32)
    final_state, outputs = lax.scan(advance, start_state, (shaped(acceptance_entries), shaped(address_entry_tile), shaped(content_entries), shaped(fading_exponent_log)))
    outputs = outputs.transpose(1, 0, 2, 3).reshape(-1, group_count_all, group_breadth)
    normed = group_norm(outputs, group_scaling_factor, group_scaling_offset, gate_rows)
    prompt_sum = head_sum(normed, w_output)
    prompt_hidden = (prompt_sum * live_mask).astype(jnp.bfloat16).reshape(prompt_count, length, model_width)
    select = (positions == request_valid_count[:, None] - 1).astype(jnp.float32)
    last_tokens = lax.optimization_barrier(jnp.sum(request_hidden_entries.astype(jnp.float32) * select[..., None], axis=1)).astype(jnp.bfloat16)
    fresh_mask = place_newness_marks == 1
    prior = jnp.where(fresh_mask[:, None], jnp.zeros_like(preceding_hidden_entry), preceding_hidden_entry)
    acceptance_each_group, address_each_group, value_per_head, decay_d, gate_d = make_inputs(newest_symbol_hidden, prior, symbol_blending_factors, w_recept, w_key, w_value, w_gate, fading_narrowing_matrix, fading_widening_matrix, feature_fading_speed)

    def blocked(array):
        return array.reshape((N_REQ, REQ_DEV) + array.shape[1:])

    def decode_block(inputs):
        acceptance_array, address_array, content_array, w, flags, states = inputs
        acceptance_array = acceptance_array.reshape(-1, group_count_all, group_breadth)
        address_array = address_array.reshape(-1, group_count_all, group_breadth)
        content_array = content_array.reshape(-1, group_count_all, group_breadth)
        w = w.reshape(-1, group_count_all, group_breadth)
        segment_opening = jnp.where((flags == 1)[:, None, None, None], jnp.zeros_like(states), states)
        result_entry_amount = jnp.einsum('lkh,lkhs->lks', acceptance_array, segment_opening, precision=lax.Precision.HIGHEST) + lax.optimization_barrier(jnp.sum(acceptance_array * group_reward * address_array, axis=-1, keepdims=True)) * content_array
        next_state = jnp.exp(w)[..., None] * segment_opening + address_array[..., :, None] * content_array[..., None, :]
        return (result_entry_amount, next_state)
    decode_out, next_states = lax.map(decode_block, (blocked(acceptance_each_group), blocked(address_each_group), blocked(value_per_head), blocked(decay_d), blocked(place_newness_marks), blocked(place_memory_matrix)))
    decode_out = decode_out.reshape(-1, group_count_all, group_breadth)
    decode_sum = head_sum(group_norm(decode_out, group_scaling_factor, group_scaling_offset, gate_d), w_output)
    prompt_taken = jnp.zeros((newest_symbol_hidden.shape[0],), jnp.float32).at[request_destination_place].set(1.0)
    decode_hidden = (decode_sum * (1.0 - prompt_taken)[:, None]).astype(jnp.bfloat16)
    new_state = next_states.reshape(place_memory_matrix.shape).at[request_destination_place].set(final_state)
    new_shift = newest_symbol_hidden.at[request_destination_place].set(last_tokens)
    return (prompt_hidden, decode_hidden, new_state, new_shift)
```

```python
import functools

import jax
import jax.numpy as jnp
from jax import lax
from jax.experimental import pallas as pl
from jax.experimental.pallas import tpu as pltpu
from jax.sharding import PartitionSpec as P

NORM_EPS = 0.00064
VMEM_LIMIT = 50 * 1024 * 1024


def project(left, right):
    return jnp.dot(left, right, preferred_element_type=jnp.float32)


def contract(left, right, left_dim, right_dim):
    return lax.dot_general(
        left, right, (((left_dim,), (right_dim,)), ((), ())), preferred_element_type=jnp.float32
    )


def mixed_tokens(x_ref, mix_ref, prompt_rows, length):
    slots = (x_ref.shape[1] - prompt_rows) // 2
    mix = mix_ref[0]
    current = x_ref[0, :prompt_rows].astype(jnp.float32)
    row = lax.broadcasted_iota(jnp.int32, current.shape, 0)
    shifted = jnp.where(row % length == 0, 0.0, pltpu.roll(current, 1, 0))
    newest = x_ref[0, prompt_rows : prompt_rows + slots].astype(jnp.float32)
    prior = x_ref[0, prompt_rows + slots :].astype(jnp.float32)
    return (
        (current + (shifted - current) * mix).astype(jnp.bfloat16),
        (newest + (prior - newest) * mix).astype(jnp.bfloat16),
    )


def accumulate(x_ref, mix_ref, weight, acc, prompt_rows, length):
    @pl.when(pl.program_id(0) == 0)
    def _():
        acc[...] = jnp.zeros_like(acc)

    prompts, slots = mixed_tokens(x_ref, mix_ref, prompt_rows, length)
    acc[:prompt_rows] += project(prompts, weight)
    acc[prompt_rows:] += project(slots, weight)


def flat_weight(w_ref):
    return w_ref[...].reshape(-1, w_ref.shape[-1])


def plain_kernel(x_ref, mix_ref, w_ref, out_ref, acc, *, prompt_rows, length):
    accumulate(x_ref, mix_ref, flat_weight(w_ref), acc, prompt_rows, length)

    @pl.when(pl.program_id(0) == pl.num_programs(0) - 1)
    def _():
        out_ref[...] = acc[...].astype(out_ref.dtype)


def key_kernel(x_ref, mix_ref, w_ref, live_ref, out_ref, acc, *, prompt_rows, length):
    accumulate(x_ref, mix_ref, flat_weight(w_ref), acc, prompt_rows, length)

    @pl.when(pl.program_id(0) == pl.num_programs(0) - 1)
    def _():
        out_ref[...] = (acc[...] * live_ref[...]).astype(out_ref.dtype)


def decay_kernel(
    x_ref, mix_ref, w_ref, live_ref, widen_ref, speed_ref, out_ref, acc, *, prompt_rows, length
):
    accumulate(x_ref, mix_ref, w_ref[...], acc, prompt_rows, length)

    @pl.when(pl.program_id(0) == pl.num_programs(0) - 1)
    def _():
        lowrank = jnp.tanh(acc[...]).astype(jnp.bfloat16)
        out_ref[...] = (
            -speed_ref[...] * jnp.exp(project(lowrank, widen_ref[...])) * live_ref[...]
        )


def gate_kernel(
    x_ref, mix_ref, w_ref, normed_p_ref, normed_d_ref, out_ref, acc, *, prompt_rows, length
):
    accumulate(x_ref, mix_ref, flat_weight(w_ref), acc, prompt_rows, length)

    @pl.when(pl.program_id(0) == pl.num_programs(0) - 1)
    def _():
        u = acc[:prompt_rows]
        out_ref[:prompt_rows] = (normed_p_ref[...] * (u / (1.0 + jnp.exp(-u)))).astype(
            out_ref.dtype
        )
        u = acc[prompt_rows:]
        out_ref[prompt_rows:] = (normed_d_ref[...] * (u / (1.0 + jnp.exp(-u)))).astype(
            out_ref.dtype
        )


def mix_project(body, features, mix, weight, extras, prompt_rows, length, columns, dtype):
    blocks, all_rows, width = features.shape
    rows = prompt_rows + (all_rows - prompt_rows) // 2
    if weight.ndim == 4:
        weight_spec = pl.BlockSpec(
            (weight.shape[0], 1, weight.shape[2], weight.shape[3]), lambda h: (0, h, 0, 0)
        )
    else:
        weight_spec = pl.BlockSpec((width, weight.shape[1]), lambda h: (h, 0))
    extra_specs = [pl.BlockSpec(extra.shape, lambda h: (0, 0)) for extra in extras]
    return pl.pallas_call(
        functools.partial(body, prompt_rows=prompt_rows, length=length),
        grid=(blocks,),
        out_shape=jax.ShapeDtypeStruct((rows, columns), dtype),
        in_specs=[
            pl.BlockSpec((1, all_rows, width), lambda h: (h, 0, 0)),
            pl.BlockSpec((1, 1, width), lambda h: (h, 0, 0)),
            weight_spec,
        ]
        + extra_specs,
        out_specs=pl.BlockSpec((rows, columns), lambda h: (0, 0)),
        scratch_shapes=[pltpu.VMEM((rows, weight.shape[-1]), jnp.float32)],
        compiler_params=pltpu.CompilerParams(vmem_limit_bytes=VMEM_LIMIT),
        cost_estimate=pl.CostEstimate(
            flops=2 * rows * blocks * width * weight.shape[-1],
            bytes_accessed=2 * features.size + 2 * weight.size + 4 * rows * columns,
            transcendentals=0,
        ),
    )(features, mix, weight, *extras)


def recurrence_kernel(
    r_ref, k_ref, v_ref, w_ref, reward_ref, gain_ref, offset_ref, out_ref, final_ref, memory,
    *, breadth, span
):
    pair = 2 * breadth
    chunk = pl.program_id(1)

    @pl.when(chunk == 0)
    def _():
        memory[...] = jnp.zeros_like(memory)

    row = lax.broadcasted_iota(jnp.int32, (span, pair), 0)
    first_head = lax.broadcasted_iota(jnp.int32, (span, pair), 1) < breadth
    later = lax.broadcasted_iota(jnp.int32, (span, span), 0)
    sooner = lax.broadcasted_iota(jnp.int32, (span, span), 1)
    apart = jnp.where(later > sooner, later ^ sooner, 0)
    same_head = (lax.broadcasted_iota(jnp.int32, (pair, pair), 0) < breadth) == (
        lax.broadcasted_iota(jnp.int32, (pair, pair), 1) < breadth
    )
    ones = jnp.where(same_head, 1.0, 0.0).astype(jnp.bfloat16)

    for index in range(memory.shape[0]):
        cols = slice(index * pair, (index + 1) * pair)
        r = r_ref[:, cols].astype(jnp.float32)
        k = k_ref[:, cols].astype(jnp.float32)
        v16 = v_ref[:, cols]
        v = v16.astype(jnp.float32)
        before = jnp.zeros((span, pair), jnp.float32)
        after = jnp.zeros((span, pair), jnp.float32)
        total = w_ref[:, cols]
        scores_a = jnp.zeros((span, span), jnp.float32)
        scores_b = jnp.zeros((span, span), jnp.float32)
        step = 1
        while step < span:
            second = (row & step) != 0
            factor = jnp.where(second, r, k) * jnp.exp(jnp.where(second, before, after))
            factor16 = factor.astype(jnp.bfloat16)
            factor_a = jnp.where(first_head, factor, 0.0).astype(jnp.bfloat16)
            factor_b = jnp.where(first_head, 0.0, factor).astype(jnp.bfloat16)
            level = (apart >= step) & (apart < 2 * step)
            scores_a = jnp.where(level, contract(factor_a, factor16, 1, 1), scores_a)
            scores_b = jnp.where(level, contract(factor_b, factor16, 1, 1), scores_b)
            partner = jnp.where(second, pltpu.roll(total, step, 0), pltpu.roll(total, span - step, 0))
            before = jnp.where(second, before + partner, before)
            after = jnp.where(second, after, after + partner)
            total = total + partner
            step *= 2
        state = memory[index]
        y = jnp.where(
            first_head,
            project(scores_a.astype(jnp.bfloat16), v16),
            project(scores_b.astype(jnp.bfloat16), v16),
        )
        y += contract((r * jnp.exp(before)).astype(jnp.bfloat16), state.astype(jnp.bfloat16), 1, 1)
        y += project((r * reward_ref[:, cols] * k).astype(jnp.bfloat16), ones) * v
        kept = (k * jnp.exp(after)).astype(jnp.bfloat16)
        memory[index] = state * jnp.exp(total[:1]) + jnp.where(
            same_head, contract(v16, kept, 0, 0), 0.0
        )
        high = y.astype(jnp.bfloat16)
        low = (y - high.astype(jnp.float32)).astype(jnp.bfloat16)
        center = y - (project(high, ones) + project(low, ones)) * (1.0 / breadth)
        spread = project((center * center).astype(jnp.bfloat16), ones) * (1.0 / breadth)
        out_ref[:, cols] = (
            center * lax.rsqrt(spread + NORM_EPS) * gain_ref[:, cols] + offset_ref[:, cols]
        )

    @pl.when(chunk == pl.num_programs(1) - 1)
    def _():
        for index in range(memory.shape[0]):
            turned = memory[index].T
            final_ref[0, 2 * index] = turned[:breadth, :breadth]
            final_ref[0, 2 * index + 1] = turned[breadth:, breadth:]


def recurrence(r, k, v, w, reward, gain, offset, prompt_count, length, breadth):
    columns = r.shape[1]
    span = min(128, length)
    chunks = length // span
    rows_spec = pl.BlockSpec((span, columns), lambda p, c: (p * chunks + c, 0))
    vector_spec = pl.BlockSpec((1, columns), lambda p, c: (0, 0))
    heads = columns // breadth
    return pl.pallas_call(
        functools.partial(recurrence_kernel, breadth=breadth, span=span),
        grid=(prompt_count, chunks),
        out_shape=(
            jax.ShapeDtypeStruct((prompt_count * length, columns), jnp.float32),
            jax.ShapeDtypeStruct((prompt_count, heads, breadth, breadth), jnp.float32),
        ),
        in_specs=[rows_spec] * 4 + [vector_spec] * 3,
        out_specs=(
            rows_spec,
            pl.BlockSpec((1, heads, breadth, breadth), lambda p, c: (p, 0, 0, 0)),
        ),
        scratch_shapes=[pltpu.VMEM((heads // 2, 2 * breadth, 2 * breadth), jnp.float32)],
        compiler_params=pltpu.CompilerParams(vmem_limit_bytes=VMEM_LIMIT),
        cost_estimate=pl.CostEstimate(
            flops=20 * prompt_count * length * columns * span,
            bytes_accessed=14 * prompt_count * length * columns,
            transcendentals=9 * prompt_count * length * columns,
        ),
    )(r, k, v, w, reward, gain, offset)


def group_norm(outputs, group_scaling_factor, group_scaling_offset):
    center = outputs - jnp.mean(outputs, axis=-1, keepdims=True)
    spread = jnp.mean(center * center, axis=-1, keepdims=True)
    normed = (center / jnp.sqrt(spread + NORM_EPS)).reshape(outputs.shape[0], -1)
    return normed * group_scaling_factor + group_scaling_offset


def on_device(
    learner_acceptance_matrix,
    learner_address_matrix,
    learner_content_matrix,
    learner_gating_matrix,
    learner_result_matrix,
    fading_narrowing_matrix,
    fading_widening_matrix,
    feature_fading_speed,
    current_reward,
    symbol_blending_factors,
    group_scaling_factor,
    group_scaling_offset,
    request_hidden_entries,
    request_valid_count,
    request_destination_place,
    newest_symbol_hidden,
    preceding_hidden_entry,
    place_memory_matrix,
    place_newness_marks,
):
    block_cols = feature_fading_speed.shape[0]
    owned_groups = place_memory_matrix.shape[1]
    group_breadth = place_memory_matrix.shape[2]
    slot_count = place_memory_matrix.shape[0]
    prompt_count, length = request_hidden_entries.shape[:2]
    prompt_rows = prompt_count * length
    blocks = lax.axis_size("head")
    fresh_mask = place_newness_marks == 1

    prior = jnp.where(fresh_mask[:, None], jnp.zeros_like(preceding_hidden_entry), preceding_hidden_entry)
    features = lax.all_gather(
        jnp.concatenate(
            [request_hidden_entries.reshape(prompt_rows, block_cols), newest_symbol_hidden, prior]
        ),
        "head",
    )
    shard_rows = learner_address_matrix.shape[0]
    shards = jnp.stack(
        [
            matrix.astype(jnp.bfloat16).reshape(shard_rows, blocks, block_cols).transpose(1, 0, 2)
            for matrix in (
                learner_address_matrix,
                learner_content_matrix,
                learner_acceptance_matrix,
                learner_gating_matrix,
            )
        ],
        axis=1,
    )
    turned = lax.all_to_all(shards, "head", 0, 0)
    w_key, w_value, w_recept, w_gate = [
        lax.all_gather(turned[:, number], "req") for number in range(4)
    ]
    w_output = lax.all_gather(learner_result_matrix.astype(jnp.bfloat16), "req", axis=0, tiled=True)

    positions = lax.broadcasted_iota(jnp.int32, (prompt_count, length), 1)
    live_mask = (positions < request_valid_count[:, None]).astype(jnp.float32).reshape(-1, 1)
    live_rows = jnp.concatenate([live_mask, jnp.ones((slot_count, 1), jnp.float32)])
    mix = symbol_blending_factors.reshape(5, blocks, 1, block_cols)
    gain = group_scaling_factor.reshape(1, -1)
    offset = group_scaling_offset.reshape(1, -1)

    def projected(body, number, weight, extras, dtype):
        return mix_project(
            body, features, mix[number], weight, extras, prompt_rows, length, block_cols, dtype
        )

    log_decay = projected(
        decay_kernel,
        3,
        fading_narrowing_matrix,
        (live_rows, fading_widening_matrix, feature_fading_speed.reshape(1, -1)),
        jnp.float32,
    )
    address = projected(key_kernel, 1, w_key, (live_rows,), jnp.bfloat16)
    content = projected(plain_kernel, 2, w_value, (), jnp.bfloat16)
    acceptance = projected(plain_kernel, 0, w_recept, (), jnp.bfloat16)
    normed_prompts, final_state = recurrence(
        acceptance,
        address,
        content,
        log_decay,
        current_reward.reshape(1, -1),
        gain,
        offset,
        prompt_count,
        length,
        group_breadth,
    )

    def slot_heads(array):
        return array[prompt_rows:].astype(jnp.float32).reshape(-1, owned_groups, group_breadth)

    slot_r, slot_k, slot_v, slot_w = [
        slot_heads(array) for array in (acceptance, address, content, log_decay)
    ]
    group_reward = current_reward.reshape(owned_groups, group_breadth)
    begin_state = jnp.where(fresh_mask[:, None, None, None], 0.0, place_memory_matrix)
    decode_out = (
        jnp.sum(slot_r[..., None] * begin_state, axis=2)
        + jnp.sum(slot_r * group_reward * slot_k, axis=-1, keepdims=True) * slot_v
    )
    new_state = (
        jnp.exp(slot_w)[..., None] * begin_state + slot_k[..., :, None] * slot_v[..., None, :]
    )
    normed_slots = group_norm(decode_out, group_scaling_factor, group_scaling_offset)
    gated = projected(gate_kernel, 4, w_gate, (normed_prompts, normed_slots), jnp.bfloat16)
    hidden = lax.psum_scatter(
        project(gated, w_output).astype(jnp.bfloat16), "head", scatter_dimension=1, tiled=True
    )
    prompt_hidden = (
        (hidden[:prompt_rows].astype(jnp.float32) * live_mask)
        .astype(jnp.bfloat16)
        .reshape(prompt_count, length, block_cols)
    )
    select = (positions == request_valid_count[:, None] - 1).astype(jnp.float32)
    last_tokens = jnp.sum(
        request_hidden_entries.astype(jnp.float32) * select[..., None], axis=1
    ).astype(jnp.bfloat16)
    offsets = request_destination_place - lax.axis_index("req") * slot_count
    slot_ids = lax.broadcasted_iota(jnp.int32, (slot_count,), 0)
    new_shift = newest_symbol_hidden
    prompt_taken = jnp.zeros((slot_count,), jnp.bool_)
    for prompt_index in range(prompt_count):
        slot_hit = slot_ids == offsets[prompt_index]
        new_state = jnp.where(slot_hit[:, None, None, None], final_state[prompt_index], new_state)
        new_shift = jnp.where(slot_hit[:, None], last_tokens[prompt_index], new_shift)
        prompt_taken = prompt_taken | slot_hit
    decode_hidden = jnp.where(
        prompt_taken[:, None], jnp.zeros((), jnp.bfloat16), hidden[prompt_rows:]
    )
    return (prompt_hidden, decode_hidden, new_state, new_shift)


def solution(mesh):
    in_specs = (
        P(("head", "req"), None),
        P(("head", "req"), None),
        P(("head", "req"), None),
        P(("head", "req"), None),
        P(("head", "req"), None),
        P(),
        P(None, "head"),
        P("head"),
        P("head"),
        P(),
        P("head"),
        P("head"),
        P("req", None, "head"),
        P("req"),
        P("req"),
        P("req", "head"),
        P("req", "head"),
        P("req", "head", None, None),
        P("req"),
    )
    out_specs = (
        P("req", None, "head"),
        P("req", "head"),
        P("req", "head", None, None),
        P("req", "head"),
    )
    return jax.shard_map(
        on_device, mesh=mesh, in_specs=in_specs, out_specs=out_specs, check_vma=False
    )
```

```python
import functools

import jax
import jax.numpy as jnp
from jax import lax
from jax.experimental import pallas as pl
from jax.experimental.pallas import tpu as pltpu
from jax.sharding import PartitionSpec as P

NORM_EPS = 0.00064
VMEM_LIMIT = 50 * 1024 * 1024


def project(left, right):
    return jnp.dot(left, right, preferred_element_type=jnp.float32)


def contract(left, right, left_dim, right_dim):
    return lax.dot_general(
        left, right, (((left_dim,), (right_dim,)), ((), ())), preferred_element_type=jnp.float32
    )


MESH = pl.DeviceIdType.MESH


def mixed_tokens(current, newest, prior, mix, length):
    current = current.astype(jnp.float32)
    row = lax.broadcasted_iota(jnp.int32, current.shape, 0)
    shifted = jnp.where(row % length == 0, 0.0, pltpu.roll(current, 1, 0))
    newest = newest.astype(jnp.float32)
    prior = prior.astype(jnp.float32)
    return (
        (current + (shifted - current) * mix).astype(jnp.bfloat16),
        (newest + (prior - newest) * mix).astype(jnp.bfloat16),
    )


def gather_project_kernel(
    features_ref,
    shards_ref,
    mix_ref,
    narrow_ref,
    widen_ref,
    speed_ref,
    live_ref,
    k_ref,
    v_ref,
    r_ref,
    w_ref,
    g_ref,
    features,
    weights,
    acc,
    low_acc,
    local_sem,
    turn_send,
    turn_recv,
    feature_send,
    feature_recv,
    outer_send,
    outer_recv,
    inner_send,
    inner_recv,
    *,
    prompt_rows,
    length,
    n_head,
    n_req,
):
    matrices = weights.shape[0]
    head = lax.axis_index("head")
    req = lax.axis_index("req")
    n_outer = n_req // 2
    partner = req + 1 - 2 * (req % 2)
    sibling = head + 1 - 2 * (head % 2)
    across = (head + n_head // 2) % n_head
    slots = (features.shape[1] - prompt_rows) // 2

    barrier = pltpu.get_barrier_semaphore()
    for d in range(1, n_head):
        pl.semaphore_signal(
            barrier, inc=1, device_id={"head": (head + d) % n_head}, device_id_type=MESH
        )
    for d in range(1, n_outer):
        pl.semaphore_signal(
            barrier, inc=1, device_id={"req": (req + 2 * d) % n_req}, device_id_type=MESH
        )
    pl.semaphore_signal(barrier, inc=1, device_id={"req": partner}, device_id_type=MESH)
    pl.semaphore_wait(barrier, n_head - 1 + n_outer)

    def turn(d):
        target = (head + d) % n_head
        return pltpu.make_async_remote_copy(
            src_ref=shards_ref.at[target],
            dst_ref=weights.at[:, req, head],
            send_sem=turn_send.at[d - 1],
            recv_sem=turn_recv.at[d - 1],
            device_id={"head": target},
            device_id_type=MESH,
        )

    def feature(block, src, target, number):
        return pltpu.make_async_remote_copy(
            src_ref=src,
            dst_ref=features.at[block],
            send_sem=feature_send.at[number],
            recv_sem=feature_recv.at[number],
            device_id={"head": target},
            device_id_type=MESH,
        )

    def outer(m, d):
        return pltpu.make_async_remote_copy(
            src_ref=weights.at[m, req],
            dst_ref=weights.at[m, req],
            send_sem=outer_send.at[m, d - 1],
            recv_sem=outer_recv.at[m, d - 1],
            device_id={"req": (req + 2 * d) % n_req},
            device_id_type=MESH,
        )

    def inner(m, d):
        block = (req - 2 * d + n_req) % n_req
        return pltpu.make_async_remote_copy(
            src_ref=weights.at[m, block],
            dst_ref=weights.at[m, block],
            send_sem=inner_send.at[m, d],
            recv_sem=inner_recv.at[m, d],
            device_id={"req": partner},
            device_id_type=MESH,
        )

    def arrived_outer(m, d):
        block = (req - 2 * d + n_req) % n_req
        pltpu.make_async_remote_copy(
            src_ref=weights.at[m, block],
            dst_ref=weights.at[m, block],
            send_sem=outer_send.at[m, d - 1],
            recv_sem=outer_recv.at[m, d - 1],
            device_id={"req": (req + 2 * d) % n_req},
            device_id_type=MESH,
        ).wait_recv()

    def arrived_inner(m, d):
        block = (partner - 2 * d + n_req) % n_req
        pltpu.make_async_remote_copy(
            src_ref=weights.at[m, block],
            dst_ref=weights.at[m, block],
            send_sem=inner_send.at[m, d],
            recv_sem=inner_recv.at[m, d],
            device_id={"req": partner},
            device_id_type=MESH,
        ).wait_recv()

    own_turn = pltpu.make_async_copy(
        shards_ref.at[head], weights.at[:, req, head], local_sem.at[0]
    )
    own_turn.start()
    for d in range(1, n_head):
        turn(d).start()
    to_across = feature(head, features_ref, across, 0)
    to_across.start()
    to_sibling = feature(head, features_ref, sibling, 1)
    to_sibling.start()
    own_features = pltpu.make_async_copy(features_ref, features.at[head], local_sem.at[1])
    own_features.start()

    own_turn.wait()
    for d in range(1, n_head):
        source = (head - d + n_head) % n_head
        pltpu.make_async_remote_copy(
            src_ref=shards_ref.at[source],
            dst_ref=weights.at[:, req, source],
            send_sem=turn_send.at[d - 1],
            recv_sem=turn_recv.at[d - 1],
            device_id={"head": source},
            device_id_type=MESH,
        ).wait_recv()
    for m in range(matrices):
        inner(m, 0).start()
        for d in range(1, n_outer):
            outer(m, d).start()

    feature(across, features_ref, across, 0).wait_recv()
    passed_on = feature(across, features.at[across], sibling, 2)
    passed_on.start()
    feature(sibling, features_ref, sibling, 1).wait_recv()
    own_features.wait()
    far = (sibling + n_head // 2) % n_head
    feature(far, features.at[far], sibling, 2).wait_recv()

    def multiply(number, weight_of, total):
        total[...] = jnp.zeros_like(total)

        @pl.loop(0, n_head)
        def _(h):
            prompts, newest = mixed_tokens(
                features[h, :prompt_rows],
                features[h, prompt_rows : prompt_rows + slots],
                features[h, prompt_rows + slots :],
                mix_ref[number, h],
                length,
            )
            weight = weight_of(h)
            total[:prompt_rows] += project(prompts, weight)
            total[prompt_rows:] += project(newest, weight)

    def forward(m):
        for d in range(1, n_outer):
            arrived_outer(m, d)
            inner(m, d).start()

    def gathered(m):
        def weight_of(h):
            return weights[m, :, h].reshape(-1, weights.shape[-1])

        return weight_of

    def landed(m):
        for d in range(n_outer):
            arrived_inner(m, d)

    multiply(3, lambda h: narrow_ref[h], low_acc)
    lowrank = jnp.tanh(low_acc[...]).astype(jnp.bfloat16)
    w_ref[...] = -speed_ref[...] * jnp.exp(project(lowrank, widen_ref[...])) * live_ref[...]

    forward(0)
    landed(0)
    for m, number in ((0, 1), (1, 2), (2, 0), (3, 4)):
        if m + 1 < matrices:
            forward(m + 1)
        multiply(number, gathered(m), acc)
        if m == 0:
            k_ref[...] = (acc[...] * live_ref[...]).astype(k_ref.dtype)
        elif m == 1:
            v_ref[...] = acc[...].astype(v_ref.dtype)
        elif m == 2:
            r_ref[...] = acc[...].astype(r_ref.dtype)
        else:
            u = acc[...]
            g_ref[...] = u / (1.0 + jnp.exp(-u))
        if m + 1 < matrices:
            landed(m + 1)

    for d in range(1, n_head):
        turn(d).wait_send()
    to_across.wait_send()
    to_sibling.wait_send()
    passed_on.wait_send()
    for m in range(matrices):
        for d in range(1, n_outer):
            outer(m, d).wait_send()
        for d in range(n_outer):
            inner(m, d).wait_send()


def gather_project(features, shards, mix, narrow, widen, speed, live, prompt_rows, length, n_req):
    n_head, matrices, shard_rows, columns = shards.shape
    all_rows = features.shape[0]
    rows = prompt_rows + (all_rows - prompt_rows) // 2
    n_outer = n_req // 2
    whole = pl.BlockSpec(memory_space=pltpu.VMEM)
    sem = pltpu.SemaphoreType.DMA
    return pl.pallas_call(
        functools.partial(
            gather_project_kernel,
            prompt_rows=prompt_rows,
            length=length,
            n_head=n_head,
            n_req=n_req,
        ),
        out_shape=(
            jax.ShapeDtypeStruct((rows, columns), jnp.bfloat16),
            jax.ShapeDtypeStruct((rows, columns), jnp.bfloat16),
            jax.ShapeDtypeStruct((rows, columns), jnp.bfloat16),
            jax.ShapeDtypeStruct((rows, columns), jnp.float32),
            jax.ShapeDtypeStruct((rows, columns), jnp.float32),
        ),
        in_specs=[whole] * 7,
        out_specs=(whole,) * 5,
        scratch_shapes=[
            pltpu.VMEM((n_head, all_rows, features.shape[1]), jnp.bfloat16),
            pltpu.VMEM((matrices, n_req, n_head, shard_rows, columns), jnp.bfloat16),
            pltpu.VMEM((rows, columns), jnp.float32),
            pltpu.VMEM((rows, narrow.shape[-1]), jnp.float32),
            sem((2,)),
            sem((n_head - 1,)),
            sem((n_head - 1,)),
            sem((3,)),
            sem((3,)),
            sem((matrices, n_outer - 1)),
            sem((matrices, n_outer - 1)),
            sem((matrices, n_outer)),
            sem((matrices, n_outer)),
        ],
        compiler_params=pltpu.CompilerParams(
            vmem_limit_bytes=VMEM_LIMIT, collective_id=0, has_side_effects=True
        ),
        cost_estimate=pl.CostEstimate(
            flops=2 * rows * n_head * features.shape[1] * columns * matrices,
            bytes_accessed=200 * 1024 * 1024,
            transcendentals=0,
        ),
    )(features, shards, mix, narrow, widen, speed, live)


def recurrence_kernel(
    r_ref, k_ref, v_ref, w_ref, g_ref, reward_ref, gain_ref, offset_ref, out_ref, final_ref, memory,
    *, breadth, span
):
    pair = 2 * breadth
    chunk = pl.program_id(1)

    @pl.when(chunk == 0)
    def _():
        memory[...] = jnp.zeros_like(memory)

    row = lax.broadcasted_iota(jnp.int32, (span, pair), 0)
    first_head = lax.broadcasted_iota(jnp.int32, (span, pair), 1) < breadth
    later = lax.broadcasted_iota(jnp.int32, (span, span), 0)
    sooner = lax.broadcasted_iota(jnp.int32, (span, span), 1)
    apart = jnp.where(later > sooner, later ^ sooner, 0)
    same_head = (lax.broadcasted_iota(jnp.int32, (pair, pair), 0) < breadth) == (
        lax.broadcasted_iota(jnp.int32, (pair, pair), 1) < breadth
    )
    ones = jnp.where(same_head, 1.0, 0.0).astype(jnp.bfloat16)

    for index in range(memory.shape[0]):
        cols = slice(index * pair, (index + 1) * pair)
        r = r_ref[:, cols].astype(jnp.float32)
        k = k_ref[:, cols].astype(jnp.float32)
        v16 = v_ref[:, cols]
        v = v16.astype(jnp.float32)
        before = jnp.zeros((span, pair), jnp.float32)
        after = jnp.zeros((span, pair), jnp.float32)
        total = w_ref[:, cols]
        scores_a = jnp.zeros((span, span), jnp.float32)
        scores_b = jnp.zeros((span, span), jnp.float32)
        step = 1
        while step < span:
            second = (row & step) != 0
            factor = jnp.where(second, r, k) * jnp.exp(jnp.where(second, before, after))
            factor16 = factor.astype(jnp.bfloat16)
            factor_a = jnp.where(first_head, factor, 0.0).astype(jnp.bfloat16)
            factor_b = jnp.where(first_head, 0.0, factor).astype(jnp.bfloat16)
            level = (apart >= step) & (apart < 2 * step)
            scores_a = jnp.where(level, contract(factor_a, factor16, 1, 1), scores_a)
            scores_b = jnp.where(level, contract(factor_b, factor16, 1, 1), scores_b)
            partner = jnp.where(second, pltpu.roll(total, step, 0), pltpu.roll(total, span - step, 0))
            before = jnp.where(second, before + partner, before)
            after = jnp.where(second, after, after + partner)
            total = total + partner
            step *= 2
        state = memory[index]
        y = jnp.where(
            first_head,
            project(scores_a.astype(jnp.bfloat16), v16),
            project(scores_b.astype(jnp.bfloat16), v16),
        )
        y += contract((r * jnp.exp(before)).astype(jnp.bfloat16), state.astype(jnp.bfloat16), 1, 1)
        y += project((r * reward_ref[:, cols] * k).astype(jnp.bfloat16), ones) * v
        kept = (k * jnp.exp(after)).astype(jnp.bfloat16)
        memory[index] = state * jnp.exp(total[:1]) + jnp.where(
            same_head, contract(v16, kept, 0, 0), 0.0
        )
        high = y.astype(jnp.bfloat16)
        low = (y - high.astype(jnp.float32)).astype(jnp.bfloat16)
        center = y - (project(high, ones) + project(low, ones)) * (1.0 / breadth)
        spread = project((center * center).astype(jnp.bfloat16), ones) * (1.0 / breadth)
        normed = center * lax.rsqrt(spread + NORM_EPS) * gain_ref[:, cols] + offset_ref[:, cols]
        out_ref[:, cols] = (normed * g_ref[:, cols]).astype(out_ref.dtype)

    @pl.when(chunk == pl.num_programs(1) - 1)
    def _():
        for index in range(memory.shape[0]):
            turned = memory[index].T
            final_ref[0, 2 * index] = turned[:breadth, :breadth]
            final_ref[0, 2 * index + 1] = turned[breadth:, breadth:]


def recurrence(r, k, v, w, g, reward, gain, offset, prompt_count, length, breadth):
    columns = r.shape[1]
    span = min(128, length)
    chunks = length // span
    rows_spec = pl.BlockSpec((span, columns), lambda p, c: (p * chunks + c, 0))
    vector_spec = pl.BlockSpec((1, columns), lambda p, c: (0, 0))
    heads = columns // breadth
    return pl.pallas_call(
        functools.partial(recurrence_kernel, breadth=breadth, span=span),
        grid=(prompt_count, chunks),
        out_shape=(
            jax.ShapeDtypeStruct((prompt_count * length, columns), jnp.bfloat16),
            jax.ShapeDtypeStruct((prompt_count, heads, breadth, breadth), jnp.float32),
        ),
        in_specs=[rows_spec] * 5 + [vector_spec] * 3,
        out_specs=(
            rows_spec,
            pl.BlockSpec((1, heads, breadth, breadth), lambda p, c: (p, 0, 0, 0)),
        ),
        scratch_shapes=[pltpu.VMEM((heads // 2, 2 * breadth, 2 * breadth), jnp.float32)],
        compiler_params=pltpu.CompilerParams(vmem_limit_bytes=VMEM_LIMIT),
        cost_estimate=pl.CostEstimate(
            flops=20 * prompt_count * length * columns * span,
            bytes_accessed=14 * prompt_count * length * columns,
            transcendentals=9 * prompt_count * length * columns,
        ),
    )(r, k, v, w, g, reward, gain, offset)


def group_norm(outputs, group_scaling_factor, group_scaling_offset):
    center = outputs - jnp.mean(outputs, axis=-1, keepdims=True)
    spread = jnp.mean(center * center, axis=-1, keepdims=True)
    normed = (center / jnp.sqrt(spread + NORM_EPS)).reshape(outputs.shape[0], -1)
    return normed * group_scaling_factor + group_scaling_offset


def on_device(
    learner_acceptance_matrix,
    learner_address_matrix,
    learner_content_matrix,
    learner_gating_matrix,
    learner_result_matrix,
    fading_narrowing_matrix,
    fading_widening_matrix,
    feature_fading_speed,
    current_reward,
    symbol_blending_factors,
    group_scaling_factor,
    group_scaling_offset,
    request_hidden_entries,
    request_valid_count,
    request_destination_place,
    newest_symbol_hidden,
    preceding_hidden_entry,
    place_memory_matrix,
    place_newness_marks,
):
    block_cols = feature_fading_speed.shape[0]
    owned_groups = place_memory_matrix.shape[1]
    group_breadth = place_memory_matrix.shape[2]
    slot_count = place_memory_matrix.shape[0]
    prompt_count, length = request_hidden_entries.shape[:2]
    prompt_rows = prompt_count * length
    blocks = lax.axis_size("head")
    fresh_mask = place_newness_marks == 1

    prior = jnp.where(fresh_mask[:, None], jnp.zeros_like(preceding_hidden_entry), preceding_hidden_entry)
    features = jnp.concatenate(
        [request_hidden_entries.reshape(prompt_rows, block_cols), newest_symbol_hidden, prior]
    )
    shard_rows = learner_address_matrix.shape[0]
    shards = jnp.stack(
        [
            matrix.astype(jnp.bfloat16).reshape(shard_rows, blocks, block_cols).transpose(1, 0, 2)
            for matrix in (
                learner_address_matrix,
                learner_content_matrix,
                learner_acceptance_matrix,
                learner_gating_matrix,
            )
        ],
        axis=1,
    )
    w_output = lax.all_gather(learner_result_matrix.astype(jnp.bfloat16), "req", axis=0, tiled=True)

    positions = lax.broadcasted_iota(jnp.int32, (prompt_count, length), 1)
    live_mask = (positions < request_valid_count[:, None]).astype(jnp.float32).reshape(-1, 1)
    live_rows = jnp.concatenate([live_mask, jnp.ones((slot_count, 1), jnp.float32)])
    mix = symbol_blending_factors.reshape(5, blocks, 1, block_cols)
    gain = group_scaling_factor.reshape(1, -1)
    offset = group_scaling_offset.reshape(1, -1)

    address, content, acceptance, log_decay, gates = gather_project(
        features,
        shards,
        mix,
        fading_narrowing_matrix.reshape(blocks, block_cols, -1),
        fading_widening_matrix,
        feature_fading_speed.reshape(1, -1),
        live_rows,
        prompt_rows,
        length,
        lax.axis_size("req"),
    )
    gated_prompts, final_state = recurrence(
        acceptance,
        address,
        content,
        log_decay,
        gates,
        current_reward.reshape(1, -1),
        gain,
        offset,
        prompt_count,
        length,
        group_breadth,
    )

    def slot_heads(array):
        return array[prompt_rows:].astype(jnp.float32).reshape(-1, owned_groups, group_breadth)

    slot_r, slot_k, slot_v, slot_w = [
        slot_heads(array) for array in (acceptance, address, content, log_decay)
    ]
    group_reward = current_reward.reshape(owned_groups, group_breadth)
    begin_state = jnp.where(fresh_mask[:, None, None, None], 0.0, place_memory_matrix)
    decode_out = (
        jnp.sum(slot_r[..., None] * begin_state, axis=2)
        + jnp.sum(slot_r * group_reward * slot_k, axis=-1, keepdims=True) * slot_v
    )
    normed_slots = group_norm(decode_out, group_scaling_factor, group_scaling_offset)
    gated_slots = (normed_slots * gates[prompt_rows:]).astype(jnp.bfloat16)
    partial_sum = project(jnp.concatenate([gated_prompts, gated_slots]), w_output).astype(
        jnp.bfloat16
    )
    partial_sum, slot_k, slot_v, slot_w = lax.optimization_barrier(
        (partial_sum, slot_k, slot_v, slot_w)
    )
    hidden = lax.psum_scatter(partial_sum, "head", scatter_dimension=1, tiled=True)
    new_state = (
        jnp.exp(slot_w)[..., None] * begin_state + slot_k[..., :, None] * slot_v[..., None, :]
    )
    prompt_hidden = (
        (hidden[:prompt_rows].astype(jnp.float32) * live_mask)
        .astype(jnp.bfloat16)
        .reshape(prompt_count, length, block_cols)
    )
    select = (positions == request_valid_count[:, None] - 1).astype(jnp.float32)
    last_tokens = jnp.sum(
        request_hidden_entries.astype(jnp.float32) * select[..., None], axis=1
    ).astype(jnp.bfloat16)
    offsets = request_destination_place - lax.axis_index("req") * slot_count
    slot_ids = lax.broadcasted_iota(jnp.int32, (slot_count,), 0)
    new_shift = newest_symbol_hidden
    prompt_taken = jnp.zeros((slot_count,), jnp.bool_)
    for prompt_index in range(prompt_count):
        slot_hit = slot_ids == offsets[prompt_index]
        new_state = jnp.where(slot_hit[:, None, None, None], final_state[prompt_index], new_state)
        new_shift = jnp.where(slot_hit[:, None], last_tokens[prompt_index], new_shift)
        prompt_taken = prompt_taken | slot_hit
    decode_hidden = jnp.where(
        prompt_taken[:, None], jnp.zeros((), jnp.bfloat16), hidden[prompt_rows:]
    )
    return (prompt_hidden, decode_hidden, new_state, new_shift)


def solution(mesh):
    in_specs = (
        P(("head", "req"), None),
        P(("head", "req"), None),
        P(("head", "req"), None),
        P(("head", "req"), None),
        P(("head", "req"), None),
        P(),
        P(None, "head"),
        P("head"),
        P("head"),
        P(),
        P("head"),
        P("head"),
        P("req", None, "head"),
        P("req"),
        P("req"),
        P("req", "head"),
        P("req", "head"),
        P("req", "head", None, None),
        P("req"),
    )
    out_specs = (
        P("req", None, "head"),
        P("req", "head"),
        P("req", "head", None, None),
        P("req", "head"),
    )
    return jax.shard_map(
        on_device, mesh=mesh, in_specs=in_specs, out_specs=out_specs, check_vma=False
    )
```

```python
import functools

import jax
import jax.numpy as jnp
from jax import lax
from jax.experimental import pallas as pl
from jax.experimental.pallas import tpu as pltpu
from jax.sharding import PartitionSpec as P

NORM_EPS = 0.00064
VMEM_LIMIT = 50 * 1024 * 1024


def project(left, right):
    return jnp.dot(left, right, preferred_element_type=jnp.float32)


def contract(left, right, left_dim, right_dim):
    return lax.dot_general(
        left, right, (((left_dim,), (right_dim,)), ((), ())), preferred_element_type=jnp.float32
    )


MESH = pl.DeviceIdType.MESH


def mixed_tokens(current, newest, prior, mix, length):
    current = current.astype(jnp.float32)
    row = lax.broadcasted_iota(jnp.int32, current.shape, 0)
    shifted = jnp.where(row % length == 0, 0.0, pltpu.roll(current, 1, 0))
    newest = newest.astype(jnp.float32)
    prior = prior.astype(jnp.float32)
    return (
        (current + (shifted - current) * mix).astype(jnp.bfloat16),
        (newest + (prior - newest) * mix).astype(jnp.bfloat16),
    )


def gather_project_kernel(
    features_ref,
    shards_ref,
    mix_ref,
    narrow_ref,
    widen_ref,
    speed_ref,
    live_ref,
    k_ref,
    v_ref,
    r_ref,
    w_ref,
    g_ref,
    features,
    weights,
    acc,
    low_acc,
    local_sem,
    turn_send,
    turn_recv,
    feature_send,
    feature_recv,
    outer_send,
    outer_recv,
    inner_send,
    inner_recv,
    *,
    prompt_rows,
    length,
    n_head,
    n_req,
):
    matrices = weights.shape[0]
    head = lax.axis_index("head")
    req = lax.axis_index("req")
    n_outer = n_req // 2
    partner = req + 1 - 2 * (req % 2)
    sibling = head + 1 - 2 * (head % 2)
    across = (head + n_head // 2) % n_head
    slots = (features.shape[1] - prompt_rows) // 2

    barrier = pltpu.get_barrier_semaphore()
    for d in range(1, n_head):
        pl.semaphore_signal(
            barrier, inc=1, device_id={"head": (head + d) % n_head}, device_id_type=MESH
        )
    for d in range(1, n_outer):
        pl.semaphore_signal(
            barrier, inc=1, device_id={"req": (req + 2 * d) % n_req}, device_id_type=MESH
        )
    pl.semaphore_signal(barrier, inc=1, device_id={"req": partner}, device_id_type=MESH)
    pl.semaphore_wait(barrier, n_head - 1 + n_outer)

    def turn(d):
        target = (head + d) % n_head
        return pltpu.make_async_remote_copy(
            src_ref=shards_ref.at[target],
            dst_ref=weights.at[:, req, head],
            send_sem=turn_send.at[d - 1],
            recv_sem=turn_recv.at[d - 1],
            device_id={"head": target},
            device_id_type=MESH,
        )

    def feature(block, src, target, number):
        return pltpu.make_async_remote_copy(
            src_ref=src,
            dst_ref=features.at[block],
            send_sem=feature_send.at[number],
            recv_sem=feature_recv.at[number],
            device_id={"head": target},
            device_id_type=MESH,
        )

    def outer(m, d):
        return pltpu.make_async_remote_copy(
            src_ref=weights.at[m, req],
            dst_ref=weights.at[m, req],
            send_sem=outer_send.at[m, d - 1],
            recv_sem=outer_recv.at[m, d - 1],
            device_id={"req": (req + 2 * d) % n_req},
            device_id_type=MESH,
        )

    def inner(m, d):
        block = (req - 2 * d + n_req) % n_req
        return pltpu.make_async_remote_copy(
            src_ref=weights.at[m, block],
            dst_ref=weights.at[m, block],
            send_sem=inner_send.at[m, d],
            recv_sem=inner_recv.at[m, d],
            device_id={"req": partner},
            device_id_type=MESH,
        )

    def arrived_outer(m, d):
        block = (req - 2 * d + n_req) % n_req
        pltpu.make_async_remote_copy(
            src_ref=weights.at[m, block],
            dst_ref=weights.at[m, block],
            send_sem=outer_send.at[m, d - 1],
            recv_sem=outer_recv.at[m, d - 1],
            device_id={"req": (req + 2 * d) % n_req},
            device_id_type=MESH,
        ).wait_recv()

    def arrived_inner(m, d):
        block = (partner - 2 * d + n_req) % n_req
        pltpu.make_async_remote_copy(
            src_ref=weights.at[m, block],
            dst_ref=weights.at[m, block],
            send_sem=inner_send.at[m, d],
            recv_sem=inner_recv.at[m, d],
            device_id={"req": partner},
            device_id_type=MESH,
        ).wait_recv()

    own_turn = pltpu.make_async_copy(
        shards_ref.at[head], weights.at[:, req, head], local_sem.at[0]
    )
    own_turn.start()
    for d in range(1, n_head):
        turn(d).start()
    to_across = feature(head, features_ref, across, 0)
    to_across.start()
    to_sibling = feature(head, features_ref, sibling, 1)
    to_sibling.start()
    own_features = pltpu.make_async_copy(features_ref, features.at[head], local_sem.at[1])
    own_features.start()

    own_turn.wait()
    for d in range(1, n_head):
        source = (head - d + n_head) % n_head
        pltpu.make_async_remote_copy(
            src_ref=shards_ref.at[source],
            dst_ref=weights.at[:, req, source],
            send_sem=turn_send.at[d - 1],
            recv_sem=turn_recv.at[d - 1],
            device_id={"head": source},
            device_id_type=MESH,
        ).wait_recv()
    for m in range(matrices):
        inner(m, 0).start()
        for d in range(1, n_outer):
            outer(m, d).start()

    feature(across, features_ref, across, 0).wait_recv()
    passed_on = feature(across, features.at[across], sibling, 2)
    passed_on.start()
    feature(sibling, features_ref, sibling, 1).wait_recv()
    own_features.wait()
    far = (sibling + n_head // 2) % n_head
    feature(far, features.at[far], sibling, 2).wait_recv()

    def multiply(number, weight_of, total):
        total[...] = jnp.zeros_like(total)

        @pl.loop(0, n_head)
        def _(h):
            prompts, newest = mixed_tokens(
                features[h, :prompt_rows],
                features[h, prompt_rows : prompt_rows + slots],
                features[h, prompt_rows + slots :],
                mix_ref[number, h],
                length,
            )
            weight = weight_of(h)
            total[:prompt_rows] += project(prompts, weight)
            total[prompt_rows:] += project(newest, weight)

    def forward(m):
        for d in range(1, n_outer):
            arrived_outer(m, d)
            inner(m, d).start()

    def gathered(m):
        def weight_of(h):
            return weights[m, :, h].reshape(-1, weights.shape[-1])

        return weight_of

    def landed(m):
        for d in range(n_outer):
            arrived_inner(m, d)

    multiply(3, lambda h: narrow_ref[h], low_acc)
    lowrank = jnp.tanh(low_acc[...]).astype(jnp.bfloat16)
    w_ref[...] = -speed_ref[...] * jnp.exp(project(lowrank, widen_ref[...])) * live_ref[...]

    forward(0)
    landed(0)
    for m, number in ((0, 1), (1, 2), (2, 0), (3, 4)):
        if m + 1 < matrices:
            forward(m + 1)
        multiply(number, gathered(m), acc)
        if m == 0:
            k_ref[...] = (acc[...] * live_ref[...]).astype(k_ref.dtype)
        elif m == 1:
            v_ref[...] = acc[...].astype(v_ref.dtype)
        elif m == 2:
            r_ref[...] = acc[...].astype(r_ref.dtype)
        else:
            u = acc[...]
            g_ref[...] = u / (1.0 + jnp.exp(-u))
        if m + 1 < matrices:
            landed(m + 1)

    for d in range(1, n_head):
        turn(d).wait_send()
    to_across.wait_send()
    to_sibling.wait_send()
    passed_on.wait_send()
    for m in range(matrices):
        for d in range(1, n_outer):
            outer(m, d).wait_send()
        for d in range(n_outer):
            inner(m, d).wait_send()


def gather_project(features, shards, mix, narrow, widen, speed, live, prompt_rows, length, n_req):
    n_head, matrices, shard_rows, columns = shards.shape
    all_rows = features.shape[0]
    rows = prompt_rows + (all_rows - prompt_rows) // 2
    n_outer = n_req // 2
    whole = pl.BlockSpec(memory_space=pltpu.VMEM)
    sem = pltpu.SemaphoreType.DMA
    return pl.pallas_call(
        functools.partial(
            gather_project_kernel,
            prompt_rows=prompt_rows,
            length=length,
            n_head=n_head,
            n_req=n_req,
        ),
        out_shape=(
            jax.ShapeDtypeStruct((rows, columns), jnp.bfloat16),
            jax.ShapeDtypeStruct((rows, columns), jnp.bfloat16),
            jax.ShapeDtypeStruct((rows, columns), jnp.bfloat16),
            jax.ShapeDtypeStruct((rows, columns), jnp.float32),
            jax.ShapeDtypeStruct((rows, columns), jnp.float32),
        ),
        in_specs=[whole] * 7,
        out_specs=(whole,) * 5,
        scratch_shapes=[
            pltpu.VMEM((n_head, all_rows, features.shape[1]), jnp.bfloat16),
            pltpu.VMEM((matrices, n_req, n_head, shard_rows, columns), jnp.bfloat16),
            pltpu.VMEM((rows, columns), jnp.float32),
            pltpu.VMEM((rows, narrow.shape[-1]), jnp.float32),
            sem((2,)),
            sem((n_head - 1,)),
            sem((n_head - 1,)),
            sem((3,)),
            sem((3,)),
            sem((matrices, n_outer - 1)),
            sem((matrices, n_outer - 1)),
            sem((matrices, n_outer)),
            sem((matrices, n_outer)),
        ],
        compiler_params=pltpu.CompilerParams(
            vmem_limit_bytes=VMEM_LIMIT, collective_id=0, has_side_effects=True
        ),
        cost_estimate=pl.CostEstimate(
            flops=2 * rows * n_head * features.shape[1] * columns * matrices,
            bytes_accessed=200 * 1024 * 1024,
            transcendentals=0,
        ),
    )(features, shards, mix, narrow, widen, speed, live)


def recurrence_kernel(
    r_ref, k_ref, v_ref, w_ref, g_ref, reward_ref, gain_ref, offset_ref, out_ref, final_ref, memory,
    *, breadth, span
):
    pair = 2 * breadth
    chunk = pl.program_id(1)

    @pl.when(chunk == 0)
    def _():
        memory[...] = jnp.zeros_like(memory)

    row = lax.broadcasted_iota(jnp.int32, (span, pair), 0)
    first_head = lax.broadcasted_iota(jnp.int32, (span, pair), 1) < breadth
    later = lax.broadcasted_iota(jnp.int32, (span, span), 0)
    sooner = lax.broadcasted_iota(jnp.int32, (span, span), 1)
    apart = jnp.where(later > sooner, later ^ sooner, 0)
    same_head = (lax.broadcasted_iota(jnp.int32, (pair, pair), 0) < breadth) == (
        lax.broadcasted_iota(jnp.int32, (pair, pair), 1) < breadth
    )
    ones = jnp.where(same_head, 1.0, 0.0).astype(jnp.bfloat16)

    for index in range(memory.shape[0]):
        cols = slice(index * pair, (index + 1) * pair)
        r = r_ref[:, cols].astype(jnp.float32)
        k = k_ref[:, cols].astype(jnp.float32)
        v16 = v_ref[:, cols]
        v = v16.astype(jnp.float32)
        before = jnp.zeros((span, pair), jnp.float32)
        after = jnp.zeros((span, pair), jnp.float32)
        total = w_ref[:, cols]
        scores_a = jnp.zeros((span, span), jnp.float32)
        scores_b = jnp.zeros((span, span), jnp.float32)
        step = 1
        while step < span:
            second = (row & step) != 0
            factor = jnp.where(second, r, k) * jnp.exp(jnp.where(second, before, after))
            factor16 = factor.astype(jnp.bfloat16)
            factor_a = jnp.where(first_head, factor, 0.0).astype(jnp.bfloat16)
            factor_b = jnp.where(first_head, 0.0, factor).astype(jnp.bfloat16)
            level = (apart >= step) & (apart < 2 * step)
            scores_a = jnp.where(level, contract(factor_a, factor16, 1, 1), scores_a)
            scores_b = jnp.where(level, contract(factor_b, factor16, 1, 1), scores_b)
            partner = jnp.where(second, pltpu.roll(total, step, 0), pltpu.roll(total, span - step, 0))
            before = jnp.where(second, before + partner, before)
            after = jnp.where(second, after, after + partner)
            total = total + partner
            step *= 2
        state = memory[index]
        y = jnp.where(
            first_head,
            project(scores_a.astype(jnp.bfloat16), v16),
            project(scores_b.astype(jnp.bfloat16), v16),
        )
        y += contract((r * jnp.exp(before)).astype(jnp.bfloat16), state.astype(jnp.bfloat16), 1, 1)
        y += project((r * reward_ref[:, cols] * k).astype(jnp.bfloat16), ones) * v
        kept = (k * jnp.exp(after)).astype(jnp.bfloat16)
        memory[index] = state * jnp.exp(total[:1]) + jnp.where(
            same_head, contract(v16, kept, 0, 0), 0.0
        )
        high = y.astype(jnp.bfloat16)
        low = (y - high.astype(jnp.float32)).astype(jnp.bfloat16)
        center = y - (project(high, ones) + project(low, ones)) * (1.0 / breadth)
        spread = project((center * center).astype(jnp.bfloat16), ones) * (1.0 / breadth)
        normed = center * lax.rsqrt(spread + NORM_EPS) * gain_ref[:, cols] + offset_ref[:, cols]
        out_ref[:, cols] = (normed * g_ref[:, cols]).astype(out_ref.dtype)

    @pl.when(chunk == pl.num_programs(1) - 1)
    def _():
        for index in range(memory.shape[0]):
            turned = memory[index].T
            final_ref[0, 2 * index] = turned[:breadth, :breadth]
            final_ref[0, 2 * index + 1] = turned[breadth:, breadth:]


def recurrence(r, k, v, w, g, reward, gain, offset, prompt, length, breadth):
    prompt_count = 1
    columns = r.shape[1]
    span = min(128, length)
    chunks = length // span
    rows_spec = pl.BlockSpec((span, columns), lambda p, c: (prompt * chunks + c, 0))
    out_spec = pl.BlockSpec((span, columns), lambda p, c: (c, 0))
    vector_spec = pl.BlockSpec((1, columns), lambda p, c: (0, 0))
    heads = columns // breadth
    return pl.pallas_call(
        functools.partial(recurrence_kernel, breadth=breadth, span=span),
        grid=(prompt_count, chunks),
        out_shape=(
            jax.ShapeDtypeStruct((prompt_count * length, columns), jnp.bfloat16),
            jax.ShapeDtypeStruct((prompt_count, heads, breadth, breadth), jnp.float32),
        ),
        in_specs=[rows_spec] * 5 + [vector_spec] * 3,
        out_specs=(
            out_spec,
            pl.BlockSpec((1, heads, breadth, breadth), lambda p, c: (p, 0, 0, 0)),
        ),
        scratch_shapes=[pltpu.VMEM((heads // 2, 2 * breadth, 2 * breadth), jnp.float32)],
        compiler_params=pltpu.CompilerParams(vmem_limit_bytes=VMEM_LIMIT),
        cost_estimate=pl.CostEstimate(
            flops=20 * prompt_count * length * columns * span,
            bytes_accessed=14 * prompt_count * length * columns,
            transcendentals=9 * prompt_count * length * columns,
        ),
    )(r, k, v, w, g, reward, gain, offset)


def group_norm(outputs, group_scaling_factor, group_scaling_offset):
    center = outputs - jnp.mean(outputs, axis=-1, keepdims=True)
    spread = jnp.mean(center * center, axis=-1, keepdims=True)
    normed = (center / jnp.sqrt(spread + NORM_EPS)).reshape(outputs.shape[0], -1)
    return normed * group_scaling_factor + group_scaling_offset


def on_device(
    learner_acceptance_matrix,
    learner_address_matrix,
    learner_content_matrix,
    learner_gating_matrix,
    learner_result_matrix,
    fading_narrowing_matrix,
    fading_widening_matrix,
    feature_fading_speed,
    current_reward,
    symbol_blending_factors,
    group_scaling_factor,
    group_scaling_offset,
    request_hidden_entries,
    request_valid_count,
    request_destination_place,
    newest_symbol_hidden,
    preceding_hidden_entry,
    place_memory_matrix,
    place_newness_marks,
):
    block_cols = feature_fading_speed.shape[0]
    owned_groups = place_memory_matrix.shape[1]
    group_breadth = place_memory_matrix.shape[2]
    slot_count = place_memory_matrix.shape[0]
    prompt_count, length = request_hidden_entries.shape[:2]
    prompt_rows = prompt_count * length
    blocks = lax.axis_size("head")
    fresh_mask = place_newness_marks == 1

    prior = jnp.where(fresh_mask[:, None], jnp.zeros_like(preceding_hidden_entry), preceding_hidden_entry)
    features = jnp.concatenate(
        [request_hidden_entries.reshape(prompt_rows, block_cols), newest_symbol_hidden, prior]
    )
    shard_rows = learner_address_matrix.shape[0]
    shards = jnp.stack(
        [
            matrix.astype(jnp.bfloat16).reshape(shard_rows, blocks, block_cols).transpose(1, 0, 2)
            for matrix in (
                learner_address_matrix,
                learner_content_matrix,
                learner_acceptance_matrix,
                learner_gating_matrix,
            )
        ],
        axis=1,
    )
    w_output = lax.all_gather(learner_result_matrix.astype(jnp.bfloat16), "req", axis=0, tiled=True)

    positions = lax.broadcasted_iota(jnp.int32, (prompt_count, length), 1)
    live_mask = (positions < request_valid_count[:, None]).astype(jnp.float32).reshape(-1, 1)
    live_rows = jnp.concatenate([live_mask, jnp.ones((slot_count, 1), jnp.float32)])
    mix = symbol_blending_factors.reshape(5, blocks, 1, block_cols)
    gain = group_scaling_factor.reshape(1, -1)
    offset = group_scaling_offset.reshape(1, -1)

    address, content, acceptance, log_decay, gates = gather_project(
        features,
        shards,
        mix,
        fading_narrowing_matrix.reshape(blocks, block_cols, -1),
        fading_widening_matrix,
        feature_fading_speed.reshape(1, -1),
        live_rows,
        prompt_rows,
        length,
        lax.axis_size("req"),
    )
    offsets = request_destination_place - lax.axis_index("req") * slot_count
    slot_ids = lax.broadcasted_iota(jnp.int32, (slot_count,), 0)
    prompt_taken = jnp.zeros((slot_count,), jnp.bool_)
    for prompt_index in range(prompt_count):
        prompt_taken = prompt_taken | (slot_ids == offsets[prompt_index])

    def prompt_rows_of(prompt_index, gain):
        return recurrence(
            acceptance,
            address,
            content,
            log_decay,
            gates,
            current_reward.reshape(1, -1),
            gain,
            offset,
            prompt_index,
            length,
            group_breadth,
        )

    def product(gated, keep):
        return (project(gated, w_output) * keep).astype(jnp.bfloat16)

    def reduced(partial_sum):
        return lax.psum_scatter(partial_sum, "head", scatter_dimension=1, tiled=True)

    hidden, final_state = [], []
    for prompt_index in range(prompt_count - 1):
        gated, state = prompt_rows_of(prompt_index, gain)
        final_state.append(state[0])
        partial_sum = product(gated, live_mask[prompt_index * length : (prompt_index + 1) * length])
        partial_sum, gain = lax.optimization_barrier((partial_sum, gain))
        hidden.append(reduced(partial_sum))

    def slot_heads(array):
        return array[prompt_rows:].astype(jnp.float32).reshape(-1, owned_groups, group_breadth)

    slot_r, slot_k, slot_v, slot_w = [
        slot_heads(array) for array in (acceptance, address, content, log_decay)
    ]
    slot_r, slot_k, slot_v, slot_w, gain = lax.optimization_barrier(
        (slot_r, slot_k, slot_v, slot_w, gain)
    )
    group_reward = current_reward.reshape(owned_groups, group_breadth)
    begin_state = jnp.where(fresh_mask[:, None, None, None], 0.0, place_memory_matrix)
    decode_out = (
        jnp.sum(slot_r[..., None] * begin_state, axis=2)
        + jnp.sum(slot_r * group_reward * slot_k, axis=-1, keepdims=True) * slot_v
    )
    normed_slots = group_norm(decode_out, group_scaling_factor, group_scaling_offset)
    gated_slots = (normed_slots * gates[prompt_rows:]).astype(jnp.bfloat16)
    gated, state = prompt_rows_of(prompt_count - 1, gain)
    final_state.append(state[0])
    if hidden:
        gated, hidden[-1] = lax.optimization_barrier((gated, hidden[-1]))
    keep = jnp.concatenate(
        [live_mask[prompt_rows - length :], jnp.where(prompt_taken, 0.0, 1.0)[:, None]]
    )
    partial_sum = product(jnp.concatenate([gated, gated_slots]), keep)
    partial_sum, slot_k, slot_v, slot_w = lax.optimization_barrier(
        (partial_sum, slot_k, slot_v, slot_w)
    )
    last = reduced(partial_sum)
    hidden.append(last[:length])
    decode_hidden = last[length:]
    prompt_hidden = jnp.stack(hidden)
    new_state = (
        jnp.exp(slot_w)[..., None] * begin_state + slot_k[..., :, None] * slot_v[..., None, :]
    )
    select = (positions == request_valid_count[:, None] - 1).astype(jnp.float32)
    last_tokens = jnp.sum(
        request_hidden_entries.astype(jnp.float32) * select[..., None], axis=1
    ).astype(jnp.bfloat16)
    new_shift = newest_symbol_hidden
    for prompt_index in range(prompt_count):
        slot_hit = slot_ids == offsets[prompt_index]
        new_state = jnp.where(slot_hit[:, None, None, None], final_state[prompt_index], new_state)
        new_shift = jnp.where(slot_hit[:, None], last_tokens[prompt_index], new_shift)
    return (prompt_hidden, decode_hidden, new_state, new_shift)


def solution(mesh):
    in_specs = (
        P(("head", "req"), None),
        P(("head", "req"), None),
        P(("head", "req"), None),
        P(("head", "req"), None),
        P(("head", "req"), None),
        P(),
        P(None, "head"),
        P("head"),
        P("head"),
        P(),
        P("head"),
        P("head"),
        P("req", None, "head"),
        P("req"),
        P("req"),
        P("req", "head"),
        P("req", "head"),
        P("req", "head", None, None),
        P("req"),
    )
    out_specs = (
        P("req", None, "head"),
        P("req", "head"),
        P("req", "head", None, None),
        P("req", "head"),
    )
    return jax.shard_map(
        on_device, mesh=mesh, in_specs=in_specs, out_specs=out_specs, check_vma=False
    )
```
